256 devices in a mesh: row: 8 (over z_hi, y), col: 8 (over z_lo, core), depth: 4 (over x).
Axes of the slice: x: 4, y: 4, z: 8 (z_hi: 2, z_lo: 4; z = z_hi * 4 + z_lo), core: 2. Of those that a mesh axis runs over, the one named last changes fastest.
Arguments:
- inputs: bfloat16 [512, 14848], P(('depth', 'row'), 'col'), may hold values from -0.59765625 to 0.59765625
- preact: bfloat16 [512, 16384], P(('depth', 'col'), 'row'), may hold values from -6 to 6
- grad_out: bfloat16 [512, 14848], P(('depth', 'row'), 'col'), may hold values from -1.796875 to 1.796875
- w_in: bfloat16 [16384, 14848], P(('row', 'depth'), 'col'), may hold values from -0.046875 to 0.046875
- w_out: bfloat16 [14848, 16384], P(('col', 'depth'), 'row'), may hold values from -0.046875 to 0.046875
Outputs:
- grad_in: bfloat16 [512, 14848], P(('depth', 'row'), 'col')
- grad_w_in: bfloat16 [16384, 14848], P(('row', 'depth'), 'col')
- grad_w_out: bfloat16 [14848, 16384], P(('col', 'depth'), 'row')
The draws below stay inside these ranges and needn't reach their ends.
All inputs are finite; a program needn't handle non-finite values.
Results may differ from the reference program's by a relative error of at most 0.025.
Values may be sent and summed in bfloat16 or wider, within the bound.
No kernel may reach another device: no remote copies, remote signals or barrier semaphores. Data moves between devices by JAX's collectives and lax.ppermute only.
A program may use at most 64 MiB of HBM per device.

```python
import jax
import jax.numpy as jnp

D = 14848
HID = 16384
TOK = 512
N_DEPTH = 4


def shard_levels(stream_key, extent, split, least, largest):
    loudness, own = 1.0, jax.random.fold_in(stream_key, 6)
    for dim, shards_of in split:
        heights = jnp.exp(jax.random.uniform(jax.random.fold_in(own, dim), (shards_of,), jnp.float32, least / len(split), largest / len(split)))
        loudness = loudness * jnp.repeat(heights, extent[dim] // shards_of).reshape([-1 if axis == dim else 1 for axis in range(len(extent))])
    return loudness


def gaussian(stream_key, dims, spread, limit, cuts=(), kind=jnp.bfloat16):
    result = jax.random.normal(stream_key, dims, jnp.float32) * spread
    if len(cuts) > 0:
        result = shard_levels(stream_key, dims, cuts, -0.22, 0.18) * result
    return jnp.clip(result, min=-limit, max=limit).astype(kind)


def setup_inputs(seed: int = 0) -> dict:
    key_of = jax.random.split(jax.random.key(seed), 6)
    inputs = gaussian(key_of[0], (TOK, D), 0.1, 0.59765625, ((0, 32), (1, 8)))
    preact = gaussian(key_of[1], (TOK, HID), 1.0, 6.0, ((0, 32), (1, 8)))
    grad_out = gaussian(key_of[2], (TOK, D), 0.3, 1.796875, ((0, 32), (1, 8)))
    w_in = gaussian(key_of[3], (HID, D), D ** -0.5, 0.046875, ((0, 32), (1, 8)))
    w_out = gaussian(key_of[4], (D, HID), HID ** -0.5, 0.046875, ((0, 32), (1, 8)))
    return dict(inputs=inputs, preact=preact, grad_out=grad_out, w_in=w_in, w_out=w_out)


def group_sum(left, right, groups):
    rows = left.shape[0] // groups
    total = jnp.zeros((left.shape[1], right.shape[1]), jnp.float32)
    for group in range(groups):
        part = jnp.dot(left[group * rows:(group + 1) * rows].T, right[group * rows:(group + 1) * rows], preferred_element_type=jnp.float32)
        total = total + part.astype(jnp.bfloat16).astype(jnp.float32)
    return total.astype(jnp.bfloat16)


def reference(inputs, preact, grad_out, w_in, w_out):
    act_grad = jnp.dot(grad_out, w_out, preferred_element_type=jnp.float32)
    pre_value = preact.astype(jnp.float32)
    normal_cdf = 0.5 * (1.0 + jax.scipy.special.erf(pre_value * 0.7071067811865476))
    density = jnp.exp(-0.5 * pre_value * pre_value) * 0.3989422804014327
    hid_grad = (act_grad * (normal_cdf + pre_value * density)).astype(jnp.bfloat16)
    act_value = (pre_value * normal_cdf).astype(jnp.bfloat16)
    grad_in = jnp.dot(hid_grad, w_in, preferred_element_type=jnp.float32).astype(jnp.bfloat16)
    grad_w_in = group_sum(hid_grad, inputs, N_DEPTH)
    grad_w_out = group_sum(grad_out, act_value, N_DEPTH)
    return grad_in, grad_w_in, grad_w_out
```

```python
import jax
import jax.numpy as jnp
from jax import lax
from jax.experimental.layout import Layout, with_layout_constraint
from jax.sharding import Mesh, PartitionSpec as P

AXES = ("zh", "y", "zl", "core", "xa", "xb")
ZH, Y, ZL, CORE, XA, XB = 2, 4, 4, 2, 2, 2
X = XA * XB
DEPTH = ("xa", "xb")
ROWS = Layout(major_to_minor=(0, 1))


def flip(value, axes, bits, size):
    return lax.ppermute(value, axes, [(i, i ^ bits) for i in range(size)])


def dot(left, right):
    return jnp.dot(left, right, preferred_element_type=jnp.float32)


def over_tokens(left, right):
    return lax.dot_general(
        left, right, (((0,), (0,)), ((), ())), preferred_element_type=jnp.float32
    )


def exchange(blocks, axes):
    return lax.all_to_all(blocks, axes, 0, 0, tiled=True)


def added(blocks):
    return jnp.sum(blocks.astype(jnp.float32), axis=0)


def ordered(mine, other, index):
    first = jnp.where(index == 0, mine, other)
    second = jnp.where(index == 0, other, mine)
    return jnp.stack([first, second])


def after(value, other):
    return lax.optimization_barrier((value, other))[0]


def pick(blocks, index):
    return lax.dynamic_index_in_dim(blocks, index, 0, keepdims=False)


def relative(blocks, index):
    return jnp.stack([pick(blocks, index ^ k) for k in range(blocks.shape[0])])


def body(inputs, preact, grad_out, w_in, w_out):
    zh, y, zl = lax.axis_index("zh"), lax.axis_index("y"), lax.axis_index("zl")
    core, x = lax.axis_index("core"), lax.axis_index(DEPTH)
    rows, feats = grad_out.shape
    hid = preact.shape[1]
    part = feats // X
    hid_part = hid // X

    pre_value = preact.astype(jnp.float32)
    normal_cdf = 0.5 * (1.0 + jax.scipy.special.erf(pre_value * 0.7071067811865476))
    density = jnp.exp(-0.5 * pre_value * pre_value) * 0.3989422804014327
    slope = normal_cdf + pre_value * density
    act_rows = (pre_value * normal_cdf).astype(jnp.bfloat16)
    slope, act_rows = lax.optimization_barrier((slope, act_rows))

    dy, x_rows = lax.optimization_barrier(
        (flip(grad_out, "zh", 1, ZH), flip(inputs, "zh", 1, ZH))
    )
    dy = ordered(grad_out, dy, zh)
    x_rows = ordered(inputs, x_rows, zh)

    dy = dy.reshape(ZH, rows, X, part).transpose(2, 0, 1, 3)
    dy = jnp.broadcast_to(dy, (Y,) + dy.shape).reshape(Y * X, ZH * rows, part)
    dy, *x_far = lax.optimization_barrier(
        [exchange(dy, ("y",) + DEPTH)] + [flip(x_rows, DEPTH, k, X) for k in (1, 2, 3)]
    )
    x_rows = jnp.stack([x_rows] + x_far).reshape(-1, feats)
    dy = dy.reshape(Y // 2, 2, X, ZH, rows, part)
    dy = dy.transpose(1, 2, 3, 0, 4, 5).reshape(CORE, X * ZL * rows, part)

    theirs = dot(pick(dy, 1 - core), w_out).astype(jnp.bfloat16)
    theirs = flip(theirs, "core", 1, CORE)
    sums = dot(pick(dy, core), w_out) + theirs.astype(jnp.float32)
    sums = sums.astype(jnp.bfloat16).reshape(X, ZL * rows, hid)
    x_rows = after(x_rows, sums)
    sums, x_one, x_three = lax.optimization_barrier(
        (exchange(sums, DEPTH), flip(x_rows, "y", 1, Y), flip(x_rows, "y", 3, Y))
    )
    sums = added(sums).astype(jnp.bfloat16).reshape(ZL, rows, hid)
    act_rows = after(act_rows, sums)
    act_grad, *act_far = lax.optimization_barrier(
        [exchange(sums, ("zl",))] + [flip(act_rows, DEPTH, k, X) for k in (1, 2, 3)]
    )
    act_rows = jnp.concatenate([act_rows] + act_far)

    hid_grad = (added(act_grad) * slope).astype(jnp.bfloat16)
    dz = hid_grad.reshape(rows, X, 1, hid_part).transpose(1, 2, 0, 3)
    dz = jnp.broadcast_to(dz, (X, ZL, rows, hid_part)).reshape(X * ZL, rows, hid_part)
    act_rows, x_rows = after((act_rows, x_rows), dz)
    dz, x_two, act_one = lax.optimization_barrier(
        (
            exchange(dz, DEPTH + ("zl",)),
            flip(x_rows, "y", 2, Y),
            flip(act_rows, "zl", 1, ZL),
        )
    )
    dz = ordered(dz, flip(dz, "core", 1, CORE), core)
    dz = dz.reshape(CORE, X, ZH, Y // 2, rows, hid_part)
    dz = dz.transpose(3, 0, 1, 2, 4, 5).reshape(-1, hid_part)

    total = with_layout_constraint(dot(dz, w_in).astype(jnp.bfloat16), ROWS)
    total = total.reshape(Y * X, ZH * rows, feats)
    act_rows = after(act_rows, total)

    dz = relative(dz.reshape(Y, X, ZH * rows, hid_part), y)
    dz = jnp.stack([pick(dz.transpose(1, 0, 2, 3), x ^ k) for k in range(X)], 1)
    dz = dz.reshape(-1, hid_part)
    x_rows = jnp.concatenate([x_rows, x_one, x_two, x_three])
    grad_w_in = over_tokens(dz, x_rows).astype(jnp.bfloat16)

    total, act_two, act_three = lax.optimization_barrier(
        (
            exchange(total, ("y",) + DEPTH),
            flip(act_rows, "zl", 2, ZL),
            flip(act_rows, "zl", 3, ZL),
        )
    )
    total = added(total).reshape(ZH, rows, feats)
    theirs = flip(pick(total, 1 - zh).astype(jnp.bfloat16), "zh", 1, ZH)
    grad_in = (pick(total, zh) + theirs.astype(jnp.float32)).astype(jnp.bfloat16)

    act_rows = jnp.concatenate([act_rows, act_one, act_two, act_three])
    act_far = flip(act_rows, "core", 1, CORE)
    dy = dy.reshape(CORE, X, ZL, rows, part)
    dy = jnp.stack([pick(dy.transpose(1, 0, 2, 3, 4), x ^ k) for k in range(X)], 1)
    dy = dy.transpose(2, 0, 1, 3, 4)
    dy = relative(dy, zl).transpose(1, 0, 2, 3, 4)
    near = pick(dy, core).reshape(-1, part)
    far = pick(dy, 1 - core).reshape(-1, part)
    grad_w_out = over_tokens(near, act_rows) + over_tokens(far, act_far)
    return (grad_in, grad_w_in, grad_w_out.astype(jnp.bfloat16))


def solution(mesh):
    fine = Mesh(mesh.devices.reshape(ZH, Y, ZL, CORE, XA, XB), AXES)
    row, col = ("zh", "y"), ("zl", "core")
    return jax.shard_map(
        body,
        mesh=fine,
        in_specs=(
            P(DEPTH + row, col),
            P(DEPTH + col, row),
            P(DEPTH + row, col),
            P(row + DEPTH, col),
            P(col + DEPTH, row),
        ),
        out_specs=(
            P(DEPTH + row, col),
            P(row + DEPTH, col),
            P(col + DEPTH, row),
        ),
        check_vma=False,
    )
```

```python
import jax
import jax.numpy as jnp
from jax import lax
from jax.experimental.layout import Layout, with_layout_constraint
from jax.sharding import Mesh, PartitionSpec as P

AXES = ("zh", "y", "zl", "core", "xa", "xb")
ZH, Y, ZL, CORE, XA, XB = 2, 4, 4, 2, 2, 2
X = XA * XB
DEPTH = ("xa", "xb")
ROWS = Layout(major_to_minor=(0, 1))


def flip(value, axes, bits, size):
    return lax.ppermute(value, axes, [(i, i ^ bits) for i in range(size)])


def dot(left, right):
    return jnp.dot(left, right, preferred_element_type=jnp.float32)


def wide(value):
    return value.astype(jnp.float32)


def over_tokens(left, right):
    return lax.dot_general(
        left, right, (((0,), (0,)), ((), ())), preferred_element_type=jnp.float32
    )


def exchange(blocks, axes):
    return lax.all_to_all(blocks, axes, 0, 0, tiled=True)


def added(blocks):
    return jnp.sum(wide(blocks), axis=0)


def ordered(mine, other, index):
    first = jnp.where(index == 0, mine, other)
    second = jnp.where(index == 0, other, mine)
    return jnp.stack([first, second])


def beside(*transfers):
    return lax.optimization_barrier(transfers)


def after(value, other):
    return lax.optimization_barrier((value, other))[0]


def pick(blocks, index):
    return lax.dynamic_index_in_dim(blocks, index, 0, keepdims=False)


def relative(blocks, index):
    return jnp.stack([pick(blocks, index ^ k) for k in range(blocks.shape[0])])


def plus(mine, others):
    return sum((wide(other) for other in others), wide(mine))


def body(inputs, preact, grad_out, w_in, w_out):
    zh, y, zl = lax.axis_index("zh"), lax.axis_index("y"), lax.axis_index("zl")
    core, x = lax.axis_index("core"), lax.axis_index(DEPTH)
    rows, feats = grad_out.shape
    hid = preact.shape[1]
    part = feats // X
    hid_part = hid // X

    def over_x(value, k):
        return flip(value, DEPTH, k, X)

    def over_y(value, k):
        return flip(value, "y", k, Y)

    pre_value = wide(preact)
    normal_cdf = 0.5 * (1.0 + jax.scipy.special.erf(pre_value * 0.7071067811865476))
    density = jnp.exp(-0.5 * pre_value * pre_value) * 0.3989422804014327
    slope = normal_cdf + pre_value * density
    act = (pre_value * normal_cdf).astype(jnp.bfloat16)
    slope, act = lax.optimization_barrier((slope, act))

    dy = ordered(grad_out, flip(grad_out, "zh", 1, ZH), zh)
    act_send = after(act, dy)
    x_pair = jnp.stack([inputs, flip(inputs, "zh", 1, ZH)])

    dy = dy.reshape(ZH, rows, X, part).transpose(2, 0, 1, 3)
    dy = jnp.broadcast_to(dy, (Y,) + dy.shape).reshape(Y * X, ZH * rows, part)
    dy, x_far, act_far = beside(
        exchange(dy, ("y",) + DEPTH),
        [over_x(x_pair, k) for k in (1, 2, 3)],
        [flip(act_send, "zl", k, ZL) for k in (1, 2, 3)],
    )
    x_rows = jnp.stack([x_pair] + x_far).reshape(-1, feats)
    act = jnp.concatenate([act] + act_far)
    dy = dy.reshape(Y // 2, 2, X, ZH, rows, part)
    dy = dy.transpose(1, 2, 3, 0, 4, 5).reshape(CORE, X, ZL * rows, part)

    dy_x = relative(dy.transpose(1, 0, 2, 3), x).transpose(1, 0, 2, 3)
    dy_x = dy_x.reshape(CORE, X * ZL * rows, part)
    theirs = dot(pick(dy_x, 1 - core), w_out).astype(jnp.bfloat16)
    sums = dot(pick(dy_x, core), w_out) + wide(flip(theirs, "core", 1, CORE))
    sums = sums.astype(jnp.bfloat16).reshape(X, ZL * rows, hid)
    sums, x_rows = lax.optimization_barrier((sums, x_rows))

    y_rows = after(x_rows, sums)
    others, x_one, x_three = beside(
        [over_x(sums[k], k) for k in (1, 2, 3)], over_y(y_rows, 1), over_y(y_rows, 3)
    )
    sums = plus(sums[0], others).astype(jnp.bfloat16).reshape(ZL, rows, hid)

    send = after(act, sums)
    act_grad, act_one, act_three = beside(
        exchange(sums, ("zl",)), over_x(send, 1), over_x(send, 3)
    )

    hid_grad = (added(act_grad) * slope).astype(jnp.bfloat16)
    dz = hid_grad.reshape(rows, X, 1, hid_part).transpose(1, 2, 0, 3)
    dz = jnp.broadcast_to(dz, (X, ZL, rows, hid_part)).reshape(X * ZL, rows, hid_part)
    dz, x_two, act_two = beside(
        exchange(dz, DEPTH + ("zl",)),
        over_y(after(x_rows, dz), 2),
        over_x(after(act, dz), 2),
    )
    dz = ordered(dz, flip(dz, "core", 1, CORE), core)
    dz = dz.reshape(CORE, X, ZH, Y // 2, rows, hid_part)
    dz = dz.transpose(3, 0, 1, 2, 4, 5).reshape(Y, X, ZH, rows, hid_part)
    dz = relative(relative(dz, y).transpose(1, 0, 2, 3, 4), x).transpose(2, 0, 1, 3, 4)
    own, far = pick(dz, zh), pick(dz, 1 - zh).transpose(1, 0, 2, 3)
    dz = jnp.stack([own, far]).reshape(-1, hid_part)

    total = with_layout_constraint(dot(dz, w_in).astype(jnp.bfloat16), ROWS)
    total = total.reshape(2, 4, 4 * rows, feats)

    dz = jnp.stack([own.transpose(1, 0, 2, 3), far], 2).reshape(-1, hid_part)
    x_rows = jnp.concatenate([x_rows, x_one, x_two, x_three])
    grad_w_in = over_tokens(dz, x_rows).astype(jnp.bfloat16)

    act = jnp.concatenate([act, act_one, act_two, act_three])
    act_far = flip(act, "core", 1, CORE)

    own, far = beside(
        [over_x(total[0, k], k) for k in (1, 2, 3)],
        [over_y(total[1, k], k) for k in (1, 2, 3)],
    )
    own = plus(total[0, 0], own).astype(jnp.bfloat16).reshape(4, rows, feats)
    far = plus(total[1, 0], far).astype(jnp.bfloat16).reshape(4, rows, feats)
    rest = beside(
        [over_y(own[k], k) for k in (1, 2, 3)], [over_x(far[k], k) for k in (1, 2, 3)]
    )
    rest, act, act_far = beside(rest, act, act_far)
    (own_rest, far_rest), grad_w_in = beside(rest, grad_w_in)
    far = flip(plus(far[0], far_rest).astype(jnp.bfloat16), "zh", 1, ZH)
    grad_in = (plus(own[0], own_rest) + wide(far)).astype(jnp.bfloat16)

    dy = dy.reshape(CORE, X, ZL, rows, part).transpose(1, 2, 0, 3, 4)
    dy = relative(relative(dy, x).transpose(1, 0, 2, 3, 4), zl).transpose(2, 1, 0, 3, 4)
    grad_w_out = over_tokens(pick(dy, core).reshape(-1, part), act)
    grad_w_out = grad_w_out + over_tokens(pick(dy, 1 - core).reshape(-1, part), act_far)
    return (grad_in, grad_w_in, grad_w_out.astype(jnp.bfloat16))


def solution(mesh):
    fine = Mesh(mesh.devices.reshape(ZH, Y, ZL, CORE, XA, XB), AXES)
    row, col = ("zh", "y"), ("zl", "core")
    return jax.shard_map(
        body,
        mesh=fine,
        in_specs=(
            P(DEPTH + row, col),
            P(DEPTH + col, row),
            P(DEPTH + row, col),
            P(row + DEPTH, col),
            P(col + DEPTH, row),
        ),
        out_specs=(
            P(DEPTH + row, col),
            P(row + DEPTH, col),
            P(col + DEPTH, row),
        ),
        check_vma=False,
    )
```

```python
import jax
import jax.numpy as jnp
from jax import lax
from jax.experimental.layout import Layout, with_layout_constraint
from jax.sharding import Mesh, PartitionSpec as P

AXES = ("zh", "y", "zl", "core", "xa", "xb")
ZH, Y, ZL, CORE, XA, XB = 2, 4, 4, 2, 2, 2
X = XA * XB
DEPTH = ("xa", "xb")
ROWS = Layout(major_to_minor=(0, 1))


def flip(value, axes, bits, size):
    return lax.ppermute(value, axes, [(i, i ^ bits) for i in range(size)])


def dot(left, right):
    return jnp.dot(left, right, preferred_element_type=jnp.float32)


def wide(value):
    return value.astype(jnp.float32)


def over_tokens(left, right):
    return lax.dot_general(
        left, right, (((0,), (0,)), ((), ())), preferred_element_type=jnp.float32
    )


def exchange(blocks, axes):
    return lax.all_to_all(blocks, axes, 0, 0, tiled=True)


def added(blocks):
    return jnp.sum(wide(blocks), axis=0)


def ordered(mine, other, index):
    first = jnp.where(index == 0, mine, other)
    second = jnp.where(index == 0, other, mine)
    return jnp.stack([first, second])


def beside(*transfers):
    return lax.optimization_barrier(transfers)


def pick(blocks, index):
    return lax.dynamic_index_in_dim(blocks, index, 0, keepdims=False)


def relative(blocks, index):
    return jnp.stack([pick(blocks, index ^ k) for k in range(blocks.shape[0])])


def plus(mine, others):
    return sum((wide(other) for other in others), wide(mine))


def body(inputs, preact, grad_out, w_in, w_out):
    zh, y, zl = lax.axis_index("zh"), lax.axis_index("y"), lax.axis_index("zl")
    core, x = lax.axis_index("core"), lax.axis_index(DEPTH)
    rows, feats = grad_out.shape
    hid = preact.shape[1]
    part = feats // X
    hid_part = hid // X

    def over_x(value, k):
        return flip(value, DEPTH, k, X)

    def over_y(value, k):
        return flip(value, "y", k, Y)

    pre_value = wide(preact)
    normal_cdf = 0.5 * (1.0 + jax.scipy.special.erf(pre_value * 0.7071067811865476))
    density = jnp.exp(-0.5 * pre_value * pre_value) * 0.3989422804014327
    slope = normal_cdf + pre_value * density
    act = (pre_value * normal_cdf).astype(jnp.bfloat16)
    slope, act = lax.optimization_barrier((slope, act))

    dy = ordered(grad_out, flip(grad_out, "zh", 1, ZH), zh)
    x_pair = jnp.stack([inputs, flip(inputs, "zh", 1, ZH)])

    dy = dy.reshape(ZH, rows, X, part).transpose(2, 0, 1, 3)
    dy = jnp.broadcast_to(dy, (Y,) + dy.shape).reshape(Y * X, ZH * rows, part)
    dy, x_far, act_far = beside(
        exchange(dy, ("y",) + DEPTH),
        [over_x(x_pair, k) for k in (1, 2, 3)],
        [flip(act, "zl", k, ZL) for k in (1, 2, 3)],
    )
    x_rows = jnp.stack([x_pair] + x_far).reshape(-1, feats)
    act = jnp.concatenate([act] + act_far)
    dy = dy.reshape(Y // 2, 2, X, ZH, rows, part)
    dy = dy.transpose(1, 2, 3, 0, 4, 5).reshape(CORE, X, ZL * rows, part)

    dy_x = relative(dy.transpose(1, 0, 2, 3), x).transpose(1, 0, 2, 3)
    dy_x = dy_x.reshape(CORE, X * ZL * rows, part)
    theirs = dot(pick(dy_x, 1 - core), w_out).astype(jnp.bfloat16)
    theirs, x_rows = beside(flip(theirs, "core", 1, CORE), x_rows)
    sums = dot(pick(dy_x, core), w_out) + wide(theirs)
    sums = sums.astype(jnp.bfloat16).reshape(X, ZL * rows, hid)

    others, x_one, x_three = beside(
        [over_x(sums[k], k) for k in (1, 2, 3)], over_y(x_rows, 1), over_y(x_rows, 3)
    )
    sums = plus(sums[0], others).astype(jnp.bfloat16).reshape(ZL, rows, hid)

    act_grad, act_one, act_three = beside(
        exchange(sums, ("zl",)), over_x(act, 1), over_x(act, 3)
    )

    hid_grad = (added(act_grad) * slope).astype(jnp.bfloat16)
    dz = hid_grad.reshape(rows, X, 1, hid_part).transpose(1, 2, 0, 3)
    dz = jnp.broadcast_to(dz, (X, ZL, rows, hid_part)).reshape(X * ZL, rows, hid_part)
    dz, x_two, act_two = beside(
        exchange(dz, DEPTH + ("zl",)),
        over_y(x_rows, 2),
        over_x(act, 2),
    )
    dz = ordered(dz, flip(dz, "core", 1, CORE), core)
    dz = dz.reshape(CORE, X, ZH, Y // 2, rows, hid_part)
    dz = dz.transpose(3, 0, 1, 2, 4, 5).reshape(Y, X, ZH, rows, hid_part)
    dz = relative(relative(dz, y).transpose(1, 0, 2, 3, 4), x).transpose(2, 0, 1, 3, 4)
    own, far = pick(dz, zh), pick(dz, 1 - zh).transpose(1, 0, 2, 3)
    dz = jnp.stack([own, far]).reshape(-1, hid_part)

    total = with_layout_constraint(dot(dz, w_in).astype(jnp.bfloat16), ROWS)
    total = total.reshape(2, 4, 4 * rows, feats)

    dz = jnp.stack([own.transpose(1, 0, 2, 3), far], 2).reshape(-1, hid_part)
    x_rows = jnp.concatenate([x_rows, x_one, x_two, x_three])
    grad_w_in = over_tokens(dz, x_rows).astype(jnp.bfloat16)

    act = jnp.concatenate([act, act_one, act_two, act_three])
    act_far = flip(act, "core", 1, CORE)

    own, far = beside(
        [over_x(total[0, k], k) for k in (1, 2, 3)],
        [over_y(total[1, k], k) for k in (1, 2, 3)],
    )
    own = plus(total[0, 0], own).astype(jnp.bfloat16).reshape(4, rows, feats)
    far = plus(total[1, 0], far).astype(jnp.bfloat16).reshape(4, rows, feats)
    rest = beside(
        [over_y(own[k], k) for k in (1, 2, 3)], [over_x(far[k], k) for k in (1, 2, 3)]
    )
    rest, act, act_far = beside(rest, act, act_far)
    (own_rest, far_rest), grad_w_in = beside(rest, grad_w_in)
    far = flip(plus(far[0], far_rest).astype(jnp.bfloat16), "zh", 1, ZH)
    grad_in = (plus(own[0], own_rest) + wide(far)).astype(jnp.bfloat16)

    dy = dy.reshape(CORE, X, ZL, rows, part).transpose(1, 2, 0, 3, 4)
    dy = relative(relative(dy, x).transpose(1, 0, 2, 3, 4), zl).transpose(2, 1, 0, 3, 4)
    grad_w_out = over_tokens(pick(dy, core).reshape(-1, part), act)
    grad_w_out = grad_w_out + over_tokens(pick(dy, 1 - core).reshape(-1, part), act_far)
    return (grad_in, grad_w_in, grad_w_out.astype(jnp.bfloat16))


def solution(mesh):
    fine = Mesh(mesh.devices.reshape(ZH, Y, ZL, CORE, XA, XB), AXES)
    row, col = ("zh", "y"), ("zl", "core")
    return jax.shard_map(
        body,
        mesh=fine,
        in_specs=(
            P(DEPTH + row, col),
            P(DEPTH + col, row),
            P(DEPTH + row, col),
            P(row + DEPTH, col),
            P(col + DEPTH, row),
        ),
        out_specs=(
            P(DEPTH + row, col),
            P(row + DEPTH, col),
            P(col + DEPTH, row),
        ),
        check_vma=False,
    )
```
